32 devices in a mesh: group: 2 (over y), train: 4 (over z), module: 4 (over x, core).
Axes of the slice: x: 2, y: 2, z: 4, core: 2. Of those that a mesh axis runs over, the one named last changes fastest.
Arguments:
- query_tokens: int32 [128, 8], P(('group', 'train')), parts along dimension 0, may hold values from 0 to 152063, as said below
- activations: bfloat16 [4, 128, 8, 5120], P('module', ('group', 'train')), parts along dimension 1, may hold values from -6 to 6
- out_grads: bfloat16 [4, 128, 8, 5120], P('module', ('group', 'train')), parts along dimension 1, may hold values from -6 to 6
- in_proj: bfloat16 [4, 5120, 64], P('module'), may hold values from -0.078125 to 0.078125
- out_proj: bfloat16 [4, 5120, 64], P('module'), may hold values from -0.078125 to 0.078125
- in_factor: float32 [4, 64, 64], P('module')
- out_factor: float32 [4, 64, 64], P('module')
- train_store: bfloat16 [4, 2048, 4096], P('module', ('group', 'train')), parts along dimension 1, may hold values from -0.375 to 0.375
- store_rows: int32 [4, 8], P('module', ('group', 'train')), parts along dimension 1, may hold values from 64 to 256, as said below
Outputs:
- scores: float32 [128, 1024], P('group', ('train', 'module')), parts along dimension 0
The draws below stay inside these ranges and needn't reach their ends.
There are 2 independent parts, one for each index of `group`. The reference program is written for one: setup_inputs(seed, part) draws one part's arguments, and reference() takes and returns one part's arrays. A program takes and returns all parts, laid end to end along the dimension named above; an argument that names none is the same for every part. Nothing has to cross between parts.
Inputs may be any that keep to these rules, and one draw needn't show every extreme that they name: `query_tokens`: 0 marks padding, which fills a tail of each query; each query has at least 4 and fewer than 8 real tokens. `store_rows`: rows of a store shard at or past its count hold stale data.
All inputs are finite; a program needn't handle non-finite values.
Results may differ from the reference program's by a relative error of at most 0.0029.
Values may be sent and summed in bfloat16 or wider, within the bound.
A program may use at most 64 MiB of HBM per device.

```python
import jax
import jax.numpy as jnp
from jax import lax

D = 5120
VOCAB = 152064
RANK = 64
QTOK = 8
TRAIN_DEV = 256
MODULES = 4
STORES = 4
QUERIES = 64
TRAIN = 1024


def factor_matrix(key):
    key_diag, key_off = jax.random.split(key)
    diag = jnp.exp(jax.random.uniform(key_diag, (MODULES, RANK), jnp.float32, -0.7, 0.7))
    off = 0.3 * jax.random.normal(key_off, (MODULES, RANK, RANK), jnp.float32) / RANK ** 0.5
    sym = 0.5 * (off + jnp.swapaxes(off, 1, 2))
    eye = jnp.eye(RANK, dtype=jnp.float32)
    return (sym * (1.0 - eye)[None] + diag[:, :, None] * eye[None]).astype(jnp.float32)


def draw_in_factor(key, part):
    return factor_matrix(jax.random.fold_in(key, 11))


def draw_out_factor(key, part):
    return factor_matrix(jax.random.fold_in(key, 23))


def draw_query_tokens(key, part):
    key_len, key_ids = jax.random.split(jax.random.fold_in(key, 5))
    lengths = jax.random.randint(key_len, (QUERIES, 1), QTOK // 2, QTOK, dtype=jnp.int32)
    values = jax.random.randint(key_ids, (QUERIES, QTOK), 1, VOCAB, dtype=jnp.int32)
    places = jnp.arange(QTOK, dtype=jnp.int32)[None, :]
    values = jnp.where(places < lengths, values, 0)
    return values.at[0, 0].set(VOCAB - 1)


def draw_store_rows(key, part):
    key_val, key_pick = jax.random.split(jax.random.fold_in(key, 7))
    values = jax.random.randint(key_val, (MODULES, STORES), TRAIN_DEV // 4, TRAIN_DEV + 1, dtype=jnp.int32)
    picked = jax.random.randint(key_pick, (MODULES, 1), 0, STORES, dtype=jnp.int32)
    shards = jnp.arange(STORES, dtype=jnp.int32)[None, :]
    values = jnp.where(shards == picked, TRAIN_DEV, values)
    values = jnp.where(shards == (picked + 1) % STORES, TRAIN_DEV // 4, values)
    return values


def steps_of(stream_key, extent, cuts, low, high):
    def one(position, parts):
        heights = jax.random.uniform(jax.random.fold_in(jax.random.fold_in(stream_key, 6), position), (parts,), jnp.float32, low / len(cuts), high / len(cuts))
        return jnp.repeat(jnp.exp(heights), extent[position] // parts).reshape((-1,) + (1,) * (len(extent) - position - 1))

    level = one(*cuts[0])
    for cut in cuts[1:]:
        level = level * one(*cut)
    return level


def noise(stream_key, extent, scale, limit, cuts=(), held_as=jnp.bfloat16):
    result = jax.random.normal(stream_key, extent, jnp.float32) * scale
    if len(cuts) > 0:
        result = steps_of(stream_key, extent, cuts, -0.22, 0.18) * result
    return jnp.clip(result, min=-limit, max=limit).astype(held_as)


def setup_inputs(seed: int = 0, part: int = 0) -> dict:
    key_list = jax.random.split(jax.random.key(seed), 10)
    part_splits = jax.random.split(jax.random.fold_in(key_list[9], part), 10)
    return {
        "query_tokens": draw_query_tokens(jax.random.fold_in(jax.random.fold_in(key_list[9], part), 71), part),
        "activations": noise(part_splits[1], (MODULES, QUERIES, QTOK, D), 1.0, 6.0, ((0, 4), (1, 4))),
        "out_grads": noise(part_splits[2], (MODULES, QUERIES, QTOK, D), 1.0, 6.0, ((0, 4), (1, 4))),
        "in_proj": noise(key_list[3], (MODULES, D, RANK), D ** -0.5, 0.078125, ((0, 4),)),
        "out_proj": noise(key_list[4], (MODULES, D, RANK), D ** -0.5, 0.078125, ((0, 4),)),
        "in_factor": draw_in_factor(jax.random.fold_in(key_list[9], 71), part),
        "out_factor": draw_out_factor(jax.random.fold_in(key_list[9], 71), part),
        "train_store": noise(part_splits[7], (MODULES, TRAIN, RANK * RANK), 0.0625, 0.375, ((0, 4), (1, 4))),
        "store_rows": draw_store_rows(jax.random.fold_in(jax.random.fold_in(key_list[9], part), 71), part),
    }


def precondition(token_ids, acts, grads, in_proj, out_proj, in_factor, out_factor):
    keep = (token_ids > 0).astype(jnp.float32)
    counted = jnp.sum(keep, axis=1)
    xin = jnp.dot(acts.reshape(QUERIES * QTOK, D), in_proj, preferred_element_type=jnp.float32)
    xin = xin.reshape(QUERIES, QTOK, RANK)
    gout = jnp.dot(grads.reshape(QUERIES * QTOK, D), out_proj, preferred_element_type=jnp.float32)
    gout = gout.reshape(QUERIES, QTOK, RANK) * keep[:, :, None]
    grad = jnp.einsum("qto,qti->qoi", gout, xin, precision=lax.Precision.HIGHEST) / counted[:, None, None]
    left = jnp.einsum("ab,qbi->qai", out_factor, grad, precision=lax.Precision.HIGHEST)
    both = jnp.einsum("qai,ic->qac", left, in_factor, precision=lax.Precision.HIGHEST)
    return both.reshape(QUERIES, RANK * RANK).astype(jnp.bfloat16)


def reference(query_tokens, activations, out_grads, in_proj, out_proj, in_factor, out_factor, train_store, store_rows):
    rows_all = jnp.arange(TRAIN, dtype=jnp.int32)
    within = rows_all % TRAIN_DEV
    owner = rows_all // TRAIN_DEV
    total = jnp.zeros((QUERIES, TRAIN), jnp.float32)
    for module in range(MODULES):
        pre = precondition(query_tokens, activations[module], out_grads[module], in_proj[module],
                           out_proj[module], in_factor[module], out_factor[module])
        valid = (within < store_rows[module][owner]).astype(jnp.float32)
        product = jnp.dot(pre, train_store[module].T, preferred_element_type=jnp.float32)
        total = total + product * valid[None, :]
    return total
```

```python
import functools
import math

import jax
import jax.numpy as jnp
from jax import lax
from jax.experimental import pallas as pl
from jax.experimental.pallas import tpu as pltpu
from jax.sharding import PartitionSpec as P

MESH = pl.DeviceIdType.MESH
HIGH = lax.Precision.HIGHEST
NT = (((1,), (1,)), ((), ()))
CHUNKS = 4


def onehot(condition):
    return jnp.where(condition, 1.0, 0.0).astype(jnp.bfloat16)


def kernel(
    n,
    m,
    tok_hbm,
    acts_hbm,
    grads_hbm,
    inp_hbm,
    outp_hbm,
    inf_hbm,
    outf_hbm,
    store_hbm,
    rows,
    out_ref,
    tok,
    acts,
    grads,
    inp,
    outp,
    inf,
    outf,
    store,
    spread,
    uv,
    held,
    pre,
    part,
    parts_in,
    load_sem,
    small_sem,
    send_sem,
    recv_sem,
    psend_sem,
    precv_sem,
):
    slots, queries = tok.shape
    used = slots - 1
    rank, width = inp.shape
    wide = rank * rank
    share = out_ref.shape[1]
    group = part.shape[3] // queries
    me = lax.axis_index("train")
    mod = lax.axis_index("module")
    step = width // CHUNKS

    loads = []
    for c in range(CHUNKS):
        at = pl.ds(c * step, step)
        row = []
        for i, (src, dst) in enumerate(
            ((grads_hbm, grads), (outp_hbm, outp), (acts_hbm, acts), (inp_hbm, inp))
        ):
            copy = pltpu.make_async_copy(src.at[:, at], dst.at[:, at], load_sem.at[c, i])
            copy.start()
            row.append(copy)
        loads.append(row)
    smalls = []
    for i, (src, dst) in enumerate(
        ((tok_hbm, tok), (outf_hbm, outf), (inf_hbm, inf), (store_hbm, store))
    ):
        copy = pltpu.make_async_copy(src, dst, small_sem.at[i])
        copy.start()
        smalls.append(copy)

    barrier = pltpu.get_barrier_semaphore()

    def greet(k, carry):
        pl.semaphore_signal(
            barrier, inc=1, device_id={"train": lax.rem(me + k, n)}, device_id_type=MESH
        )
        return carry

    lax.fori_loop(1, n, greet, 0, unroll=n <= 4)
    for k in range(1, m):
        pl.semaphore_signal(
            barrier, inc=1, device_id={"module": lax.rem(mod + k, m)}, device_id_type=MESH
        )

    k_at = lax.broadcasted_iota(jnp.int32, (4 * rank, wide), 0) % (2 * rank)
    n_at = lax.broadcasted_iota(jnp.int32, (4 * rank, wide), 1) // rank
    spread[:, 0:wide] = onehot(k_at == n_at)
    k_at = lax.broadcasted_iota(jnp.int32, (4 * rank, 2 * rank), 0) % (2 * rank)
    n_at = lax.broadcasted_iota(jnp.int32, (4 * rank, 2 * rank), 1) % rank
    spread[:, wide : wide + 2 * rank] = onehot(k_at == n_at + rank)

    smalls[0].wait()
    keep = onehot(tok[...] > 0)
    r_at = lax.broadcasted_iota(jnp.int32, (slots * queries, queries), 0)
    q_at = lax.broadcasted_iota(jnp.int32, (slots * queries, queries), 1)
    of_query = lax.dot_general(
        onehot(r_at % queries == q_at), keep, NT, preferred_element_type=jnp.float32
    )
    counted = jnp.sum(of_query, axis=1, keepdims=True)
    r_at = lax.broadcasted_iota(jnp.int32, (slots * queries, slots), 0)
    t_at = lax.broadcasted_iota(jnp.int32, (slots * queries, slots), 1)
    kept = jnp.sum(jnp.where(r_at // queries == t_at, of_query, 0.0), axis=1, keepdims=True)
    lane = lax.broadcasted_iota(jnp.int32, (slots * queries, 2 * rank), 1)
    weight = jnp.where(lane < rank, kept / counted, 1.0)

    gout = jnp.zeros((slots * queries, rank), jnp.float32)
    xin = jnp.zeros((slots * queries, rank), jnp.float32)
    for c in range(CHUNKS):
        at = slice(c * step, (c + 1) * step)
        loads[c][0].wait()
        loads[c][1].wait()
        gout += lax.dot_general(grads[:, at], outp[:, at], NT, preferred_element_type=jnp.float32)
        loads[c][2].wait()
        loads[c][3].wait()
        xin += lax.dot_general(acts[:, at], inp[:, at], NT, preferred_element_type=jnp.float32)

    smalls[1].wait()
    smalls[2].wait()
    uv[:, 0:rank] = lax.dot_general(
        gout, outf[...], NT, precision=HIGH, preferred_element_type=jnp.float32
    )
    uv[:, rank : 2 * rank] = jnp.dot(
        xin, inf[...], precision=HIGH, preferred_element_type=jnp.float32
    )
    for t in range(used):
        at = slice(t * queries, (t + 1) * queries)
        both = uv[pl.ds(t, queries, stride=slots), :] * weight[at]
        high = both.astype(jnp.bfloat16)
        low = (both - high.astype(jnp.float32)).astype(jnp.bfloat16)
        held[me, at, 0 : 2 * rank] = high
        held[me, at, 2 * rank : 4 * rank] = low

    pl.semaphore_wait(barrier, n - 1 + m - 1)

    def exchange(k):
        return pltpu.make_async_remote_copy(
            src_ref=held.at[me],
            dst_ref=held.at[me],
            send_sem=send_sem.at[k],
            recv_sem=recv_sem.at[k],
            device_id={"train": lax.rem(me + k, n)},
            device_id_type=MESH,
        )

    def send(k, carry):
        exchange(k).start()
        return carry

    lax.fori_loop(1, n, send, 0, unroll=n <= 4)

    def expand(s):
        block = held[s]
        v = jnp.dot(
            block, spread[:, wide : wide + 2 * rank], preferred_element_type=jnp.float32
        )
        v = jnp.concatenate([v, v], axis=1)
        for j in range(wide // (4 * rank)):
            at = slice(j * 4 * rank, (j + 1) * 4 * rank)
            u = jnp.dot(block, spread[:, at], preferred_element_type=jnp.float32)
            prod = u * v
            total = prod[0:queries]
            for t in range(1, used):
                total += prod[t * queries : (t + 1) * queries]
            pre[s // group, pl.ds(pl.multiple_of((s % group) * queries, queries), queries), at] = (
                total.astype(jnp.bfloat16)
            )

    expand(me)

    def arrive(k, carry):
        pltpu.make_async_copy(held.at[me], held.at[me], recv_sem.at[k]).wait()
        expand(lax.rem(me - k + n, n))
        return carry

    lax.fori_loop(1, n, arrive, 0)

    smalls[3].wait()
    r_at = lax.broadcasted_iota(jnp.int32, (store.shape[0], 1), 0)
    valid = r_at < rows[0, 0]

    def score(b, carry):
        product = lax.dot_general(store[...], pre[b], NT, preferred_element_type=jnp.float32)
        product = jnp.where(valid, product, 0.0)
        for j in range(m):
            part[j, b] = product[j * share : (j + 1) * share]
        return carry

    blocks = n // group
    lax.fori_loop(0, blocks, score, 0, unroll=blocks == 1)

    def reduce(k):
        to = lax.rem(mod + k, m)
        return pltpu.make_async_remote_copy(
            src_ref=part.at[to],
            dst_ref=parts_in.at[k],
            send_sem=psend_sem.at[k],
            recv_sem=precv_sem.at[k],
            device_id={"module": to},
            device_id_type=MESH,
        )

    for k in range(1, m):
        reduce(k).start()

    def sent(k, carry):
        exchange(k).wait_send()
        return carry

    lax.fori_loop(1, n, sent, 0, unroll=n <= 4)
    for k in range(1, m):
        reduce(k).wait_recv()

    def finish(b, carry):
        total = part[mod, b]
        for k in range(1, m):
            total += parts_in[k, b]
        size = group * queries
        out_ref[pl.ds(pl.multiple_of(b * size, size), size), :] = total.T
        return carry

    lax.fori_loop(0, blocks, finish, 0, unroll=blocks == 1)
    for k in range(1, m):
        reduce(k).wait_send()


def on_device(
    n,
    m,
    query_tokens,
    activations,
    out_grads,
    in_proj,
    out_proj,
    in_factor,
    out_factor,
    train_store,
    store_rows,
):
    queries, slots = query_tokens.shape
    width, rank = in_proj.shape[1:]
    count, wide = train_store.shape[1:]
    share = count // m
    group = math.gcd(n, 4)
    blocks = n // group
    bf16, f32, i32 = jnp.bfloat16, jnp.float32, jnp.int32
    scratch = [
        pltpu.VMEM((slots, queries), i32),
        pltpu.VMEM((queries * slots, width), bf16),
        pltpu.VMEM((queries * slots, width), bf16),
        pltpu.VMEM((rank, width), bf16),
        pltpu.VMEM((rank, width), bf16),
        pltpu.VMEM((rank, rank), f32),
        pltpu.VMEM((rank, rank), f32),
        pltpu.VMEM((count, wide), bf16),
        pltpu.VMEM((4 * rank, wide + 2 * rank), bf16),
        pltpu.VMEM((queries * slots, 2 * rank), f32),
        pltpu.VMEM((n, (slots - 1) * queries, 4 * rank), bf16),
        pltpu.VMEM((blocks, group * queries, wide), bf16),
        pltpu.VMEM((m, blocks, share, group * queries), f32),
        pltpu.VMEM((m, blocks, share, group * queries), f32),
        pltpu.SemaphoreType.DMA((CHUNKS, 4)),
        pltpu.SemaphoreType.DMA((4,)),
        pltpu.SemaphoreType.DMA((n,)),
        pltpu.SemaphoreType.DMA((n,)),
        pltpu.SemaphoreType.DMA((m,)),
        pltpu.SemaphoreType.DMA((m,)),
    ]
    return pl.pallas_call(
        functools.partial(kernel, n, m),
        out_shape=jax.ShapeDtypeStruct((n * queries, share), f32),
        in_specs=[pl.BlockSpec(memory_space=pl.ANY)] * 8 + [pl.BlockSpec(memory_space=pltpu.SMEM)],
        out_specs=pl.BlockSpec(memory_space=pltpu.VMEM),
        scratch_shapes=scratch,
        compiler_params=pltpu.CompilerParams(
            collective_id=0, has_side_effects=True, vmem_limit_bytes=56 * 1024 * 1024
        ),
    )(
        query_tokens.T,
        activations.reshape(queries * slots, width),
        out_grads.reshape(queries * slots, width),
        jnp.swapaxes(in_proj[0], 0, 1),
        jnp.swapaxes(out_proj[0], 0, 1),
        in_factor[0],
        out_factor[0],
        train_store[0],
        store_rows,
    )


def solution(mesh):
    placed = (
        P(("group", "train"), None),
        P("module", ("group", "train"), None, None),
        P("module", ("group", "train"), None, None),
        P("module", None, None),
        P("module", None, None),
        P("module", None, None),
        P("module", None, None),
        P("module", ("group", "train"), None),
        P("module", ("group", "train")),
    )
    return jax.shard_map(
        functools.partial(on_device, mesh.shape["train"], mesh.shape["module"]),
        mesh=mesh,
        in_specs=placed,
        out_specs=P("group", ("train", "module")),
        check_vma=False,
    )
```

```python
import functools
import math

import jax
import jax.numpy as jnp
from jax import lax
from jax.experimental import pallas as pl
from jax.experimental.pallas import tpu as pltpu
from jax.sharding import PartitionSpec as P

MESH = pl.DeviceIdType.MESH
HIGH = lax.Precision.HIGHEST
NT = (((1,), (1,)), ((), ()))
CHUNKS = 4


def onehot(condition):
    return jnp.where(condition, 1.0, 0.0).astype(jnp.bfloat16)


def kernel(
    n,
    m,
    tok_hbm,
    acts_hbm,
    grads_hbm,
    inp_hbm,
    outp_hbm,
    inf_hbm,
    outf_hbm,
    store_hbm,
    rows,
    out_ref,
    tok,
    acts,
    grads,
    inp,
    outp,
    inf,
    outf,
    store,
    spread,
    uv,
    held,
    pre,
    part,
    parts_in,
    load_sem,
    small_sem,
    send_sem,
    recv_sem,
    psend_sem,
    precv_sem,
):
    slots, queries = tok.shape
    used = slots - 1
    rank, width = inp.shape
    wide = rank * rank
    share = out_ref.shape[1]
    group = part.shape[3] // (2 * queries)
    me = lax.axis_index("train")
    mod = lax.axis_index("module")
    step = width // CHUNKS

    barrier = pltpu.get_barrier_semaphore()

    def greet(k, carry):
        pl.semaphore_signal(
            barrier, inc=1, device_id={"train": lax.rem(me + k, n)}, device_id_type=MESH
        )
        return carry

    lax.fori_loop(1, n, greet, 0, unroll=n <= 4)
    for k in range(1, m):
        pl.semaphore_signal(
            barrier, inc=1, device_id={"module": lax.rem(mod + k, m)}, device_id_type=MESH
        )

    smalls = []
    for i, (src, dst) in enumerate(
        ((tok_hbm, tok), (outf_hbm, outf), (inf_hbm, inf))
    ):
        copy = pltpu.make_async_copy(src, dst, small_sem.at[i])
        copy.start()
        smalls.append(copy)
    loads = []
    for i, pair in enumerate((((grads_hbm, grads), (outp_hbm, outp)), ((acts_hbm, acts), (inp_hbm, inp)))):
        column = []
        for c in range(CHUNKS):
            at = pl.ds(c * step, step)
            row = []
            for h, (src, dst) in enumerate(pair):
                copy = pltpu.make_async_copy(
                    src.at[:, at], dst.at[:, at], load_sem.at[i, c, h]
                )
                copy.start()
                row.append(copy)
            column.append(row)
        loads.append(column)
    copy = pltpu.make_async_copy(store_hbm, store, small_sem.at[3])
    copy.start()
    smalls.append(copy)

    k_at = lax.broadcasted_iota(jnp.int32, (2 * rank, wide), 0) % rank
    n_at = lax.broadcasted_iota(jnp.int32, (2 * rank, wide), 1) // rank
    spread[:, 0:wide] = onehot(k_at == n_at)
    k_at = lax.broadcasted_iota(jnp.int32, (2 * rank, 2 * rank), 0) % rank
    n_at = lax.broadcasted_iota(jnp.int32, (2 * rank, 2 * rank), 1) % rank
    spread[:, wide : wide + 2 * rank] = onehot(k_at == n_at)

    smalls[0].wait()
    keep = onehot(tok[...] > 0)
    r_at = lax.broadcasted_iota(jnp.int32, (slots * queries, queries), 0)
    q_at = lax.broadcasted_iota(jnp.int32, (slots * queries, queries), 1)
    of_query = lax.dot_general(
        onehot(r_at % queries == q_at), keep, NT, preferred_element_type=jnp.float32
    )
    counted = jnp.sum(of_query, axis=1, keepdims=True)
    r_at = lax.broadcasted_iota(jnp.int32, (slots * queries, slots), 0)
    t_at = lax.broadcasted_iota(jnp.int32, (slots * queries, slots), 1)
    kept = jnp.sum(jnp.where(r_at // queries == t_at, of_query, 0.0), axis=1, keepdims=True)
    weight = kept / counted

    smalls[1].wait()
    smalls[2].wait()

    def exchange(i, k):
        return pltpu.make_async_remote_copy(
            src_ref=held.at[me, i],
            dst_ref=held.at[me, i],
            send_sem=send_sem.at[i, k],
            recv_sem=recv_sem.at[i, k],
            device_id={"train": lax.rem(me + k, n)},
            device_id_type=MESH,
        )

    for i, (left, right) in enumerate(((grads, outp), (acts, inp))):
        total = jnp.zeros((slots * queries, rank), jnp.float32)
        for c in range(CHUNKS):
            at = slice(c * step, (c + 1) * step)
            loads[i][c][0].wait()
            loads[i][c][1].wait()
            total += lax.dot_general(
                left[:, at], right[:, at], NT, preferred_element_type=jnp.float32
            )
        factor = outf[...].T if i == 0 else inf[...]
        total = jnp.dot(total, factor, precision=HIGH, preferred_element_type=jnp.float32)
        uv[:, 0:rank] = total
        uv[:, rank : 2 * rank] = total
        lane = lax.broadcasted_iota(jnp.int32, (queries, 2 * rank), 1)
        for t in range(used):
            at = slice(t * queries, (t + 1) * queries)
            both = uv[pl.ds(t, queries, stride=slots), :]
            if i == 0:
                both = both * weight[at]
            high = both.astype(jnp.bfloat16).astype(jnp.float32)
            held[me, i, at, :] = jnp.where(lane < rank, high, both - high).astype(jnp.bfloat16)
        if i == 0:
            pl.semaphore_wait(barrier, n - 1 + m - 1)

        def send(k, carry):
            exchange(i, k).start()
            return carry

        lax.fori_loop(1, n, send, 0, unroll=n <= 4)

    def expand(s):
        block = held[s, 0]
        v = jnp.dot(
            held[s, 1], spread[:, wide : wide + 2 * rank], preferred_element_type=jnp.float32
        )
        v = jnp.concatenate([v, v], axis=1)
        for j in range(wide // (4 * rank)):
            at = slice(j * 4 * rank, (j + 1) * 4 * rank)
            u = jnp.dot(block, spread[:, at], preferred_element_type=jnp.float32)
            prod = u * v
            total = prod[0:queries]
            for t in range(1, used):
                total += prod[t * queries : (t + 1) * queries]
            pre[s // group, pl.ds(pl.multiple_of((s % group) * queries, queries), queries), at] = (
                total.astype(jnp.bfloat16)
            )

    expand(me)

    def arrive(k, carry):
        exchange(0, k).wait_recv()
        exchange(1, k).wait_recv()
        expand(lax.rem(me - k + n, n))
        return carry

    lax.fori_loop(1, n, arrive, 0)

    smalls[3].wait()
    r_at = lax.broadcasted_iota(jnp.int32, (store.shape[0], 1), 0)
    valid = r_at < rows[0, 0]

    def score(b, carry):
        product = lax.dot_general(store[...], pre[b], NT, preferred_element_type=jnp.float32)
        product = jnp.where(valid, product, 0.0)
        for j in range(m):
            part[j, b] = jnp.concatenate(
                [
                    product[j * share : j * share + share // 2],
                    product[j * share + share // 2 : (j + 1) * share],
                ],
                axis=1,
            )
        return carry

    blocks = n // group
    lax.fori_loop(0, blocks, score, 0, unroll=blocks == 1)

    def reduce(k):
        to = lax.rem(mod + k, m)
        return pltpu.make_async_remote_copy(
            src_ref=part.at[to],
            dst_ref=parts_in.at[k],
            send_sem=psend_sem.at[k],
            recv_sem=precv_sem.at[k],
            device_id={"module": to},
            device_id_type=MESH,
        )

    for k in range(1, m):
        reduce(k).start()

    def sent(k, carry):
        exchange(0, k).wait_send()
        exchange(1, k).wait_send()
        return carry

    lax.fori_loop(1, n, sent, 0, unroll=n <= 4)
    for k in range(1, m):
        reduce(k).wait_recv()

    def finish(b, carry):
        total = part[mod, b]
        for k in range(1, m):
            total += parts_in[k, b]
        size = group * queries
        total = jnp.concatenate([total[:, 0:size], total[:, size : 2 * size]], axis=0)
        out_ref[pl.ds(pl.multiple_of(b * size, size), size), :] = total.T
        return carry

    lax.fori_loop(0, blocks, finish, 0, unroll=blocks == 1)
    for k in range(1, m):
        reduce(k).wait_send()


def on_device(
    n,
    m,
    query_tokens,
    activations,
    out_grads,
    in_proj,
    out_proj,
    in_factor,
    out_factor,
    train_store,
    store_rows,
):
    queries, slots = query_tokens.shape
    width, rank = in_proj.shape[1:]
    count, wide = train_store.shape[1:]
    share = count // m
    group = math.gcd(n, 4)
    blocks = n // group
    bf16, f32, i32 = jnp.bfloat16, jnp.float32, jnp.int32
    scratch = [
        pltpu.VMEM((slots, queries), i32),
        pltpu.VMEM((queries * slots, width), bf16),
        pltpu.VMEM((queries * slots, width), bf16),
        pltpu.VMEM((rank, width), bf16),
        pltpu.VMEM((rank, width), bf16),
        pltpu.VMEM((rank, rank), f32),
        pltpu.VMEM((rank, rank), f32),
        pltpu.VMEM((count, wide), bf16),
        pltpu.VMEM((2 * rank, wide + 2 * rank), bf16),
        pltpu.VMEM((queries * slots, 2 * rank), f32),
        pltpu.VMEM((n, 2, (slots - 1) * queries, 2 * rank), bf16),
        pltpu.VMEM((blocks, group * queries, wide), bf16),
        pltpu.VMEM((m, blocks, share // 2, 2 * group * queries), f32),
        pltpu.VMEM((m, blocks, share // 2, 2 * group * queries), f32),
        pltpu.SemaphoreType.DMA((2, CHUNKS, 2)),
        pltpu.SemaphoreType.DMA((4,)),
        pltpu.SemaphoreType.DMA((2, n)),
        pltpu.SemaphoreType.DMA((2, n)),
        pltpu.SemaphoreType.DMA((m,)),
        pltpu.SemaphoreType.DMA((m,)),
    ]
    return pl.pallas_call(
        functools.partial(kernel, n, m),
        out_shape=pltpu.VMEM((n * queries, share), f32),
        in_specs=[pl.BlockSpec(memory_space=pl.ANY)] * 8 + [pl.BlockSpec(memory_space=pltpu.SMEM)],
        out_specs=pl.BlockSpec(memory_space=pltpu.VMEM),
        scratch_shapes=scratch,
        compiler_params=pltpu.CompilerParams(
            collective_id=0, has_side_effects=True, vmem_limit_bytes=56 * 1024 * 1024
        ),
    )(
        query_tokens.T,
        activations.reshape(queries * slots, width),
        out_grads.reshape(queries * slots, width),
        jnp.swapaxes(in_proj[0], 0, 1),
        jnp.swapaxes(out_proj[0], 0, 1),
        in_factor[0],
        out_factor[0],
        train_store[0],
        store_rows,
    )


def solution(mesh):
    placed = (
        P(("group", "train"), None),
        P("module", ("group", "train"), None, None),
        P("module", ("group", "train"), None, None),
        P("module", None, None),
        P("module", None, None),
        P("module", None, None),
        P("module", None, None),
        P("module", ("group", "train"), None),
        P("module", ("group", "train")),
    )
    return jax.shard_map(
        functools.partial(on_device, mesh.shape["train"], mesh.shape["module"]),
        mesh=mesh,
        in_specs=placed,
        out_specs=P("group", ("train", "module")),
        check_vma=False,
    )
```

```python
import functools
import math

import jax
import jax.numpy as jnp
from jax import lax
from jax.experimental import pallas as pl
from jax.experimental.pallas import tpu as pltpu
from jax.sharding import PartitionSpec as P

MESH = pl.DeviceIdType.MESH
HIGH = lax.Precision.HIGHEST
NT = (((1,), (1,)), ((), ()))
CHUNKS = 1


def onehot(condition):
    return jnp.where(condition, 1.0, 0.0).astype(jnp.bfloat16)


def kernel(
    n,
    m,
    tok_hbm,
    acts_hbm,
    grads_hbm,
    inp_hbm,
    outp_hbm,
    inf_hbm,
    outf_hbm,
    store_hbm,
    rows,
    out_ref,
    tok,
    acts,
    grads,
    inp,
    outp,
    inf,
    outf,
    store,
    spread,
    uv,
    held,
    pre,
    part,
    parts_in,
    load_sem,
    small_sem,
    send_sem,
    recv_sem,
    psend_sem,
    precv_sem,
):
    slots, queries = tok.shape
    used = slots - 1
    rank, width = inp.shape
    wide = rank * rank
    share = out_ref.shape[1]
    group = part.shape[3] // (2 * queries)
    me = lax.axis_index("train")
    mod = lax.axis_index("module")
    step = width // CHUNKS

    barrier = pltpu.get_barrier_semaphore()

    def greet(k, carry):
        pl.semaphore_signal(
            barrier, inc=1, device_id={"train": lax.rem(me + k, n)}, device_id_type=MESH
        )
        return carry

    lax.fori_loop(1, n, greet, 0, unroll=n <= 4)
    for k in range(1, m):
        pl.semaphore_signal(
            barrier, inc=1, device_id={"module": lax.rem(mod + k, m)}, device_id_type=MESH
        )

    smalls = []
    for i, (src, dst) in enumerate(
        ((tok_hbm, tok), (outf_hbm, outf), (inf_hbm, inf))
    ):
        copy = pltpu.make_async_copy(src, dst, small_sem.at[i])
        copy.start()
        smalls.append(copy)
    loads = []
    for i, pair in enumerate((((grads_hbm, grads), (outp_hbm, outp)), ((acts_hbm, acts), (inp_hbm, inp)))):
        column = []
        for c in range(CHUNKS):
            at = pl.ds(c * step, step)
            row = []
            for h, (src, dst) in enumerate(pair):
                copy = pltpu.make_async_copy(
                    src.at[:, at], dst.at[:, at], load_sem.at[i, c, h]
                )
                copy.start()
                row.append(copy)
            column.append(row)
        loads.append(column)
    copy = pltpu.make_async_copy(store_hbm, store, small_sem.at[3])
    copy.start()
    smalls.append(copy)

    smalls[0].wait()
    keep = onehot(tok[...] > 0)
    r_at = lax.broadcasted_iota(jnp.int32, (slots * queries, queries), 0)
    q_at = lax.broadcasted_iota(jnp.int32, (slots * queries, queries), 1)
    of_query = lax.dot_general(
        onehot(r_at % queries == q_at), keep, NT, preferred_element_type=jnp.float32
    )
    counted = jnp.sum(of_query, axis=1, keepdims=True)
    r_at = lax.broadcasted_iota(jnp.int32, (slots * queries, slots), 0)
    t_at = lax.broadcasted_iota(jnp.int32, (slots * queries, slots), 1)
    kept = jnp.sum(jnp.where(r_at // queries == t_at, of_query, 0.0), axis=1, keepdims=True)
    weight = kept / counted

    smalls[1].wait()
    smalls[2].wait()

    def exchange(i, k):
        return pltpu.make_async_remote_copy(
            src_ref=held.at[me, i],
            dst_ref=held.at[me, i],
            send_sem=send_sem.at[i, k],
            recv_sem=recv_sem.at[i, k],
            device_id={"train": lax.rem(me + k, n)},
            device_id_type=MESH,
        )

    for i, (left, right) in enumerate(((grads, outp), (acts, inp))):
        total = jnp.zeros((slots * queries, rank), jnp.float32)
        for c in range(CHUNKS):
            at = slice(c * step, (c + 1) * step)
            loads[i][c][0].wait()
            loads[i][c][1].wait()
            total += lax.dot_general(
                left[:, at], right[:, at], NT, preferred_element_type=jnp.float32
            )
        factor = outf[...].T if i == 0 else inf[...]
        total = jnp.dot(total, factor, precision=HIGH, preferred_element_type=jnp.float32)
        uv[:, 0:rank] = total
        uv[:, rank : 2 * rank] = total
        lane = lax.broadcasted_iota(jnp.int32, (queries, 2 * rank), 1)
        for t in range(used):
            at = slice(t * queries, (t + 1) * queries)
            both = uv[pl.ds(t, queries, stride=slots), :]
            if i == 0:
                both = both * weight[at]
            high = both.astype(jnp.bfloat16).astype(jnp.float32)
            held[me, i, at, :] = jnp.where(lane < rank, high, both - high).astype(jnp.bfloat16)
        if i == 0:
            pl.semaphore_wait(barrier, n - 1 + m - 1)

        def send(k, carry):
            exchange(i, k).start()
            return carry

        lax.fori_loop(1, n, send, 0, unroll=n <= 4)

    k_at = lax.broadcasted_iota(jnp.int32, (2 * rank, wide), 0) % rank
    n_at = lax.broadcasted_iota(jnp.int32, (2 * rank, wide), 1) // rank
    spread[:, 0:wide] = onehot(k_at == n_at)
    k_at = lax.broadcasted_iota(jnp.int32, (2 * rank, 2 * rank), 0) % rank
    n_at = lax.broadcasted_iota(jnp.int32, (2 * rank, 2 * rank), 1) % rank
    spread[:, wide : wide + 2 * rank] = onehot(k_at == n_at)

    def expand(s):
        block = held[s, 0]
        v = jnp.dot(
            held[s, 1], spread[:, wide : wide + 2 * rank], preferred_element_type=jnp.float32
        )
        v = jnp.concatenate([v, v], axis=1)
        for j in range(wide // (4 * rank)):
            at = slice(j * 4 * rank, (j + 1) * 4 * rank)
            u = jnp.dot(block, spread[:, at], preferred_element_type=jnp.float32)
            prod = u * v
            total = prod[0:queries]
            for t in range(1, used):
                total += prod[t * queries : (t + 1) * queries]
            pre[s // group, pl.ds(pl.multiple_of((s % group) * queries, queries), queries), at] = (
                total.astype(jnp.bfloat16)
            )

    expand(me)

    def arrive(k, carry):
        exchange(0, k).wait_recv()
        exchange(1, k).wait_recv()
        expand(lax.rem(me - k + n, n))
        return carry

    lax.fori_loop(1, n, arrive, 0)

    smalls[3].wait()
    r_at = lax.broadcasted_iota(jnp.int32, (store.shape[0], 1), 0)
    valid = r_at < rows[0, 0]

    def score(b, carry):
        product = lax.dot_general(store[...], pre[b], NT, preferred_element_type=jnp.float32)
        product = jnp.where(valid, product, 0.0)
        for j in range(m):
            part[j, b] = jnp.concatenate(
                [
                    product[j * share : j * share + share // 2],
                    product[j * share + share // 2 : (j + 1) * share],
                ],
                axis=1,
            )
        return carry

    blocks = n // group
    lax.fori_loop(0, blocks, score, 0, unroll=blocks == 1)

    def reduce(k):
        to = lax.rem(mod + k, m)
        return pltpu.make_async_remote_copy(
            src_ref=part.at[to],
            dst_ref=parts_in.at[k],
            send_sem=psend_sem.at[k],
            recv_sem=precv_sem.at[k],
            device_id={"module": to},
            device_id_type=MESH,
        )

    for k in range(1, m):
        reduce(k).start()

    def sent(k, carry):
        exchange(0, k).wait_send()
        exchange(1, k).wait_send()
        return carry

    lax.fori_loop(1, n, sent, 0, unroll=n <= 4)
    for k in range(1, m):
        reduce(k).wait_recv()

    def finish(b, carry):
        total = part[mod, b]
        for k in range(1, m):
            total += parts_in[k, b]
        size = group * queries
        total = jnp.concatenate([total[:, 0:size], total[:, size : 2 * size]], axis=0)
        out_ref[pl.ds(pl.multiple_of(b * size, size), size), :] = total.T
        return carry

    lax.fori_loop(0, blocks, finish, 0, unroll=blocks == 1)
    for k in range(1, m):
        reduce(k).wait_send()


def on_device(
    n,
    m,
    query_tokens,
    activations,
    out_grads,
    in_proj,
    out_proj,
    in_factor,
    out_factor,
    train_store,
    store_rows,
):
    queries, slots = query_tokens.shape
    width, rank = in_proj.shape[1:]
    count, wide = train_store.shape[1:]
    share = count // m
    group = math.gcd(n, 4)
    blocks = n // group
    bf16, f32, i32 = jnp.bfloat16, jnp.float32, jnp.int32
    scratch = [
        pltpu.VMEM((slots, queries), i32),
        pltpu.VMEM((queries * slots, width), bf16),
        pltpu.VMEM((queries * slots, width), bf16),
        pltpu.VMEM((rank, width), bf16),
        pltpu.VMEM((rank, width), bf16),
        pltpu.VMEM((rank, rank), f32),
        pltpu.VMEM((rank, rank), f32),
        pltpu.VMEM((count, wide), bf16),
        pltpu.VMEM((2 * rank, wide + 2 * rank), bf16),
        pltpu.VMEM((queries * slots, 2 * rank), f32),
        pltpu.VMEM((n, 2, (slots - 1) * queries, 2 * rank), bf16),
        pltpu.VMEM((blocks, group * queries, wide), bf16),
        pltpu.VMEM((m, blocks, share // 2, 2 * group * queries), f32),
        pltpu.VMEM((m, blocks, share // 2, 2 * group * queries), f32),
        pltpu.SemaphoreType.DMA((2, CHUNKS, 2)),
        pltpu.SemaphoreType.DMA((4,)),
        pltpu.SemaphoreType.DMA((2, n)),
        pltpu.SemaphoreType.DMA((2, n)),
        pltpu.SemaphoreType.DMA((m,)),
        pltpu.SemaphoreType.DMA((m,)),
    ]
    return pl.pallas_call(
        functools.partial(kernel, n, m),
        out_shape=pltpu.VMEM((n * queries, share), f32),
        in_specs=[pl.BlockSpec(memory_space=pl.ANY)] * 8 + [pl.BlockSpec(memory_space=pltpu.SMEM)],
        out_specs=pl.BlockSpec(memory_space=pltpu.VMEM),
        scratch_shapes=scratch,
        compiler_params=pltpu.CompilerParams(
            collective_id=0, has_side_effects=True, vmem_limit_bytes=56 * 1024 * 1024
        ),
    )(
        query_tokens.T,
        activations.reshape(queries * slots, width),
        out_grads.reshape(queries * slots, width),
        jnp.swapaxes(in_proj[0], 0, 1),
        jnp.swapaxes(out_proj[0], 0, 1),
        in_factor[0],
        out_factor[0],
        train_store[0],
        store_rows,
    )


def solution(mesh):
    placed = (
        P(("group", "train"), None),
        P("module", ("group", "train"), None, None),
        P("module", ("group", "train"), None, None),
        P("module", None, None),
        P("module", None, None),
        P("module", None, None),
        P("module", None, None),
        P("module", ("group", "train"), None),
        P("module", ("group", "train")),
    )
    return jax.shard_map(
        functools.partial(on_device, mesh.shape["train"], mesh.shape["module"]),
        mesh=mesh,
        in_specs=placed,
        out_specs=P("group", ("train", "module")),
        check_vma=False,
    )
```

```python
import functools
import math

import jax
import jax.numpy as jnp
from jax import lax
from jax.experimental import pallas as pl
from jax.experimental.pallas import tpu as pltpu
from jax.sharding import PartitionSpec as P

MESH = pl.DeviceIdType.MESH
HIGH = lax.Precision.HIGHEST
NT = (((1,), (1,)), ((), ()))
CHUNKS = 1


def onehot(condition):
    return jnp.where(condition, 1.0, 0.0).astype(jnp.bfloat16)


def kernel(
    n,
    m,
    tok_hbm,
    acts_hbm,
    grads_hbm,
    inp_hbm,
    outp_hbm,
    inf_hbm,
    outf_hbm,
    store_hbm,
    rows,
    out_ref,
    tok,
    acts,
    grads,
    inp,
    outp,
    inf,
    outf,
    store,
    spread,
    uv,
    held,
    pre,
    part,
    parts_in,
    load_sem,
    small_sem,
    send_sem,
    recv_sem,
    psend_sem,
    precv_sem,
):
    slots, queries = tok.shape
    used = slots - 1
    rank, width = inp.shape
    wide = rank * rank
    share = out_ref.shape[1]
    group = part.shape[3] // (2 * queries)
    me = lax.axis_index("train")
    mod = lax.axis_index("module")
    step = width // CHUNKS

    barrier = pltpu.get_barrier_semaphore()

    def greet(k, carry):
        pl.semaphore_signal(
            barrier, inc=1, device_id={"train": lax.rem(me + k, n)}, device_id_type=MESH
        )
        return carry

    lax.fori_loop(1, n, greet, 0, unroll=n <= 4)
    for k in range(1, m):
        pl.semaphore_signal(
            barrier, inc=1, device_id={"module": lax.rem(mod + k, m)}, device_id_type=MESH
        )

    smalls = []
    for i, (src, dst) in enumerate(
        ((tok_hbm, tok), (outf_hbm, outf), (inf_hbm, inf))
    ):
        copy = pltpu.make_async_copy(src, dst, small_sem.at[i])
        copy.start()
        smalls.append(copy)
    loads = []
    for i, pair in enumerate((((grads_hbm, grads), (outp_hbm, outp)), ((acts_hbm, acts), (inp_hbm, inp)))):
        column = []
        for c in range(CHUNKS):
            at = pl.ds(c * step, step)
            row = []
            for h, (src, dst) in enumerate(pair):
                copy = pltpu.make_async_copy(
                    src.at[:, at], dst.at[:, at], load_sem.at[i, c, h]
                )
                copy.start()
                row.append(copy)
            column.append(row)
        loads.append(column)
    copy = pltpu.make_async_copy(store_hbm, store, small_sem.at[3])
    copy.start()
    smalls.append(copy)

    smalls[0].wait()
    keep = onehot(tok[...] > 0)
    r_at = lax.broadcasted_iota(jnp.int32, (slots * queries, queries), 0)
    q_at = lax.broadcasted_iota(jnp.int32, (slots * queries, queries), 1)
    of_query = lax.dot_general(
        onehot(r_at % queries == q_at), keep, NT, preferred_element_type=jnp.float32
    )
    counted = jnp.sum(of_query, axis=1, keepdims=True)
    r_at = lax.broadcasted_iota(jnp.int32, (slots * queries, slots), 0)
    t_at = lax.broadcasted_iota(jnp.int32, (slots * queries, slots), 1)
    kept = jnp.sum(jnp.where(r_at // queries == t_at, of_query, 0.0), axis=1, keepdims=True)
    weight = kept / counted

    smalls[1].wait()
    smalls[2].wait()

    def exchange(i, k):
        return pltpu.make_async_remote_copy(
            src_ref=held.at[me, i],
            dst_ref=held.at[me, i],
            send_sem=send_sem.at[i, k],
            recv_sem=recv_sem.at[i, k],
            device_id={"train": lax.rem(me + k, n)},
            device_id_type=MESH,
        )

    for i, (left, right) in enumerate(((grads, outp), (acts, inp))):
        total = jnp.zeros((slots * queries, rank), jnp.float32)
        for c in range(CHUNKS):
            at = slice(c * step, (c + 1) * step)
            loads[i][c][0].wait()
            loads[i][c][1].wait()
            total += lax.dot_general(
                left[:, at], right[:, at], NT, preferred_element_type=jnp.float32
            )
        factor = outf[...].T if i == 0 else inf[...]
        total = jnp.dot(total, factor, precision=HIGH, preferred_element_type=jnp.float32)
        uv[:, 0:rank] = total
        uv[:, rank : 2 * rank] = total
        lane = lax.broadcasted_iota(jnp.int32, (queries, 2 * rank), 1)
        for t in range(used):
            at = slice(t * queries, (t + 1) * queries)
            both = uv[pl.ds(t, queries, stride=slots), :]
            if i == 0:
                both = both * weight[at]
            high = both.astype(jnp.bfloat16).astype(jnp.float32)
            held[me, i, at, :] = jnp.where(lane < rank, high, both - high).astype(jnp.bfloat16)
        if i == 0:
            pl.semaphore_wait(barrier, n - 1 + m - 1)

        def send(k, carry):
            exchange(i, k).start()
            return carry

        lax.fori_loop(1, n, send, 0, unroll=n <= 4)

    k_at = lax.broadcasted_iota(jnp.int32, (2 * rank, wide), 0) % rank
    n_at = lax.broadcasted_iota(jnp.int32, (2 * rank, wide), 1) // rank
    spread[:, 0:wide] = onehot(k_at == n_at)
    k_at = lax.broadcasted_iota(jnp.int32, (2 * rank, 2 * rank), 0) % rank
    n_at = lax.broadcasted_iota(jnp.int32, (2 * rank, 2 * rank), 1) % rank
    spread[:, wide : wide + 2 * rank] = onehot(k_at == n_at)

    def expand(s):
        block = held[s, 0]
        v = jnp.dot(
            held[s, 1], spread[:, wide : wide + 2 * rank], preferred_element_type=jnp.float32
        )
        v = jnp.concatenate([v, v], axis=1)
        for j in range(wide // (4 * rank)):
            at = slice(j * 4 * rank, (j + 1) * 4 * rank)
            u = jnp.dot(block, spread[:, at], preferred_element_type=jnp.float32)
            prod = u * v
            total = prod[0:queries]
            for t in range(1, used):
                total += prod[t * queries : (t + 1) * queries]
            pre[s // group, pl.ds(pl.multiple_of((s % group) * queries, queries), queries), at] = (
                total.astype(jnp.bfloat16)
            )

    expand(me)

    def arrive(k, carry):
        exchange(0, k).wait_recv()
        exchange(1, k).wait_recv()
        expand(lax.rem(me - k + n, n))
        return carry

    lax.fori_loop(1, n, arrive, 0, unroll=n <= 4)

    smalls[3].wait()
    r_at = lax.broadcasted_iota(jnp.int32, (store.shape[0], 1), 0)
    valid = r_at < rows[0, 0]

    def score(b, carry):
        product = lax.dot_general(store[...], pre[b], NT, preferred_element_type=jnp.float32)
        product = jnp.where(valid, product, 0.0)
        for j in range(m):
            part[j, b] = jnp.concatenate(
                [
                    product[j * share : j * share + share // 2],
                    product[j * share + share // 2 : (j + 1) * share],
                ],
                axis=1,
            )
        return carry

    blocks = n // group
    lax.fori_loop(0, blocks, score, 0, unroll=blocks == 1)

    def reduce(k):
        to = lax.rem(mod + k, m)
        return pltpu.make_async_remote_copy(
            src_ref=part.at[to],
            dst_ref=parts_in.at[k],
            send_sem=psend_sem.at[k],
            recv_sem=precv_sem.at[k],
            device_id={"module": to},
            device_id_type=MESH,
        )

    for k in range(1, m):
        reduce(k).start()

    def sent(k, carry):
        exchange(0, k).wait_send()
        exchange(1, k).wait_send()
        return carry

    lax.fori_loop(1, n, sent, 0, unroll=n <= 4)
    for k in range(1, m):
        reduce(k).wait_recv()

    def finish(b, carry):
        total = part[mod, b]
        for k in range(1, m):
            total += parts_in[k, b]
        size = group * queries
        total = jnp.concatenate([total[:, 0:size], total[:, size : 2 * size]], axis=0)
        out_ref[pl.ds(pl.multiple_of(b * size, size), size), :] = total.T
        return carry

    lax.fori_loop(0, blocks, finish, 0, unroll=blocks == 1)
    for k in range(1, m):
        reduce(k).wait_send()


def on_device(
    n,
    m,
    query_tokens,
    activations,
    out_grads,
    in_proj,
    out_proj,
    in_factor,
    out_factor,
    train_store,
    store_rows,
):
    queries, slots = query_tokens.shape
    width, rank = in_proj.shape[1:]
    count, wide = train_store.shape[1:]
    share = count // m
    group = math.gcd(n, 4)
    blocks = n // group
    bf16, f32, i32 = jnp.bfloat16, jnp.float32, jnp.int32
    scratch = [
        pltpu.VMEM((slots, queries), i32),
        pltpu.VMEM((queries * slots, width), bf16),
        pltpu.VMEM((queries * slots, width), bf16),
        pltpu.VMEM((rank, width), bf16),
        pltpu.VMEM((rank, width), bf16),
        pltpu.VMEM((rank, rank), f32),
        pltpu.VMEM((rank, rank), f32),
        pltpu.VMEM((count, wide), bf16),
        pltpu.VMEM((2 * rank, wide + 2 * rank), bf16),
        pltpu.VMEM((queries * slots, 2 * rank), f32),
        pltpu.VMEM((n, 2, (slots - 1) * queries, 2 * rank), bf16),
        pltpu.VMEM((blocks, group * queries, wide), bf16),
        pltpu.VMEM((m, blocks, share // 2, 2 * group * queries), f32),
        pltpu.VMEM((m, blocks, share // 2, 2 * group * queries), f32),
        pltpu.SemaphoreType.DMA((2, CHUNKS, 2)),
        pltpu.SemaphoreType.DMA((4,)),
        pltpu.SemaphoreType.DMA((2, n)),
        pltpu.SemaphoreType.DMA((2, n)),
        pltpu.SemaphoreType.DMA((m,)),
        pltpu.SemaphoreType.DMA((m,)),
    ]
    return pl.pallas_call(
        functools.partial(kernel, n, m),
        out_shape=pltpu.VMEM((n * queries, share), f32),
        in_specs=[pl.BlockSpec(memory_space=pl.ANY)] * 8 + [pl.BlockSpec(memory_space=pltpu.SMEM)],
        out_specs=pl.BlockSpec(memory_space=pltpu.VMEM),
        scratch_shapes=scratch,
        compiler_params=pltpu.CompilerParams(
            collective_id=0, has_side_effects=True, vmem_limit_bytes=56 * 1024 * 1024
        ),
    )(
        query_tokens.T,
        activations.reshape(queries * slots, width),
        out_grads.reshape(queries * slots, width),
        jnp.swapaxes(in_proj[0], 0, 1),
        jnp.swapaxes(out_proj[0], 0, 1),
        in_factor[0],
        out_factor[0],
        train_store[0],
        store_rows,
    )


def solution(mesh):
    placed = (
        P(("group", "train"), None),
        P("module", ("group", "train"), None, None),
        P("module", ("group", "train"), None, None),
        P("module", None, None),
        P("module", None, None),
        P("module", None, None),
        P("module", None, None),
        P("module", ("group", "train"), None),
        P("module", ("group", "train")),
    )
    return jax.shard_map(
        functools.partial(on_device, mesh.shape["train"], mesh.shape["module"]),
        mesh=mesh,
        in_specs=placed,
        out_specs=P("group", ("train", "module")),
        check_vma=False,
    )
```
